32 devices in a mesh: gx: 4 (over z), gy: 8 (over y, x, core).
Axes of the slice: x: 2, y: 2, z: 4, core: 2. Of those that a mesh axis runs over, the one named last changes fastest.
Arguments:
- points: bfloat16 [1, 32768, 256], P(None, ('gx', 'gy')), may hold values from -16 to 16
- send_rows: int32 [1, 32, 768], P(None, ('gx', 'gy')), may hold values from 0 to 1023, as said below
- recv_slot: int32 [1, 32768], P(None, ('gx', 'gy')), may hold values from 0 to 1791, as said below
- norm1_gain: float32 [256], replicated, may hold values from 0.1 to 1.9
- qkv_weight: bfloat16 [256, 768], replicated, may hold values from -0.375 to 0.375
- proj_weight: bfloat16 [256, 256], replicated, may hold values from -0.375 to 0.375
- norm2_gain: float32 [256], replicated, may hold values from 0.1 to 1.9
- fc1_weight: bfloat16 [256, 1024], replicated, may hold values from -0.375 to 0.375
- fc2_weight: bfloat16 [1024, 256], replicated, may hold values from -0.1875 to 0.1875
- cotangent: bfloat16 [1, 32768, 256], P(None, ('gx', 'gy')), may hold values from -6 to 6
Outputs:
- block_out: bfloat16 [1, 32768, 256], P(None, ('gx', 'gy'))
- grad_points: bfloat16 [1, 32768, 256], P(None, ('gx', 'gy'))
The draws below stay inside these ranges and needn't reach their ends.
Inputs may be any that keep to these rules, and one draw needn't show every extreme that they name: `send_rows`: for every event and source device a, the first L(a) of the slots toward a - 1 and the first R(a) of the slots toward a + 1 (devices mod 32) are used; the rows they name are distinct and, with the rows that recv_slot of device a lists as its own, cover all 1024 rows of a. Unused slots name arbitrary rows. L(a) and R(a) are at most 384, and in every event some device sends exactly 384 points to its next device. `recv_slot`: for every event and destination device d, the 1024 entries of d's block are distinct: a value s < 1024 names d's own z-order row s, 1024 + c the c-th slot of device d - 1 toward d, 1408 + c the c-th slot of device d + 1 toward d (mod 32); exactly the used slots appear, so that the Hilbert order is a permutation of the z-order in which every point moves at most one device along the curve.
All inputs are finite; a program needn't handle non-finite values.
Results may differ from the reference program's by a relative error of at most 0.0054.
Values may be sent and summed in bfloat16 or wider, within the bound.
A program may use at most 128 MiB of HBM per device.

```python
import math
import jax
import jax.numpy as jnp
from jax import lax

C = 256
H = 16
FF = 1024
K = 1024
P_DEV = 1024
EVENTS = 1
HD = 256
SHIFT = 512
NPTS = 32768
CAP = 384
DEVICES = 32


def routing_plan(key, event_index):
    quarter = P_DEV // 4
    eighth = P_DEV // 8
    event_key = jax.random.fold_in(jax.random.fold_in(key, 4242), event_index)
    subkeys = jax.random.split(event_key, 4)
    device_ids = jnp.arange(DEVICES, dtype=jnp.int32)
    twist = jax.random.randint(subkeys[0], (DEVICES,), 0, eighth + 1).astype(jnp.int32)
    pinned = jax.random.randint(subkeys[1], (), 0, DEVICES).astype(jnp.int32)
    twist = jnp.where(device_ids == pinned, eighth, twist).astype(jnp.int32)
    before = twist[(device_ids - 1 + DEVICES) % DEVICES]
    left_count = quarter + before
    right_count = quarter + twist
    row_orders = jax.vmap(lambda source_id: jax.random.permutation(jax.random.fold_in(subkeys[2], source_id), P_DEV))(device_ids).astype(jnp.int32)
    slot_ids = jnp.arange(CAP, dtype=jnp.int32)
    left_rows = row_orders[:, :CAP]
    right_pos = (P_DEV - right_count[:, None] + slot_ids[None, :]) % P_DEV
    right_rows = jnp.take_along_axis(row_orders, right_pos, axis=1)
    send_table = jnp.concatenate([left_rows, right_rows], axis=1)
    rank_ids = jnp.arange(P_DEV, dtype=jnp.int32)

    def place_rows(dest_id):
        own_left = left_count[dest_id]
        keep = P_DEV - own_left - right_count[dest_id]
        from_prev = right_count[(dest_id - 1 + DEVICES) % DEVICES]
        own_rows = row_orders[dest_id][jnp.clip(own_left + rank_ids, 0, P_DEV - 1)]
        entries = jnp.where(rank_ids < keep, own_rows, jnp.where(rank_ids < keep + from_prev, P_DEV + rank_ids - keep, P_DEV + CAP + rank_ids - keep - from_prev))
        shuffle = jax.random.permutation(jax.random.fold_in(subkeys[3], dest_id), P_DEV)
        return entries[shuffle]
    slot_table = jax.vmap(place_rows)(device_ids).reshape(DEVICES * P_DEV)
    return (send_table.astype(jnp.int32), slot_table.astype(jnp.int32))


def draw_send_rows(key, part):
    return jax.vmap(lambda event_index: routing_plan(key, event_index)[0])(jnp.arange(EVENTS, dtype=jnp.int32))


def draw_recv_slot(key, part):
    return jax.vmap(lambda event_index: routing_plan(key, event_index)[1])(jnp.arange(EVENTS, dtype=jnp.int32))


def draw_points(key, part):
    subkeys = jax.random.split(jax.random.fold_in(key, 99), 2)
    row_scale = jnp.exp(jax.random.uniform(subkeys[1], (EVENTS, NPTS, 1), minval=math.log(0.5), maxval=math.log(4.0)))
    base_values = jnp.clip(jax.random.normal(subkeys[0], (EVENTS, NPTS, C)), -4.0, 4.0)
    return (base_values * row_scale).astype(jnp.float32).astype(jnp.bfloat16)


def level_of(stream_key, extent, cuts, smallest, top_value):
    def one(dim, blocks):
        heights = jax.random.uniform(jax.random.fold_in(jax.random.fold_in(stream_key, 6), dim), (blocks,), jnp.float32, smallest / len(cuts), top_value / len(cuts))
        return jnp.repeat(jnp.exp(heights), extent[dim] // blocks).reshape((-1,) + (1,) * (len(extent) - dim - 1))

    level = one(*cuts[0])
    for cut in cuts[1:]:
        level = level * one(*cut)
    return level


def normal_values(stream_key, shape, scale, bound, cuts=(), kind=jnp.bfloat16):
    factor_of = level_of(stream_key, shape, cuts, -0.22, 0.18) if cuts else 1.0
    drawn = jax.random.normal(stream_key, shape, jnp.float32) * scale * factor_of
    return jnp.minimum(jnp.maximum(drawn, -bound), bound).astype(kind)


def setup_inputs(seed: int = 0) -> dict:
    seeds = jax.random.split(jax.random.key(seed), 11)
    return {
        "points": draw_points(jax.random.fold_in(seeds[10], 71), 0),
        "send_rows": draw_send_rows(jax.random.fold_in(seeds[10], 71), 0),
        "recv_slot": draw_recv_slot(jax.random.fold_in(seeds[10], 71), 0),
        "norm1_gain": jnp.clip(1.0 + 0.18 * jax.random.normal(seeds[3], (C,), jnp.float32), 0.1, 1.9),
        "qkv_weight": normal_values(seeds[4], (C, 3 * HD), C ** -0.5, 0.375),
        "proj_weight": normal_values(seeds[5], (HD, C), HD ** -0.5, 0.375),
        "norm2_gain": jnp.clip(1.0 + 0.18 * jax.random.normal(seeds[6], (C,), jnp.float32), 0.1, 1.9),
        "fc1_weight": normal_values(seeds[7], (C, FF), C ** -0.5, 0.375),
        "fc2_weight": normal_values(seeds[8], (FF, C), FF ** -0.5, 0.1875),
        "cotangent": normal_values(seeds[9], (EVENTS, NPTS, C), 1.0, 6.0, ((1, 32),)),
    }


epsilon = 1e-05

def norm_rows(row_block, gain):
    row_mean = lax.optimization_barrier(jnp.mean(row_block, axis=-1, keepdims=True))
    centered = row_block - row_mean
    spread = lax.optimization_barrier(jnp.mean(centered * centered, axis=-1, keepdims=True))
    return centered * lax.rsqrt(spread + epsilon) * gain

def gelu_exact(values):
    return jax.nn.gelu(values, approximate=False)

def front(ordered, norm1_gain, qkv_weight):
    normed = norm_rows(ordered.astype(jnp.float32), norm1_gain).astype(jnp.bfloat16)
    return jnp.dot(normed, qkv_weight, preferred_element_type=jnp.float32).astype(jnp.bfloat16)

def rest_pass(ordered, attention, norm2_gain, proj_weight, fc1_weight, fc2_weight, cotangent):
    mixed_rows = ordered.astype(jnp.float32) + jnp.dot(attention, proj_weight, preferred_element_type=jnp.float32)
    normed_two, norm_back = jax.vjp(lambda row_block: norm_rows(row_block, norm2_gain), mixed_rows)
    hidden_pre = jnp.dot(normed_two.astype(jnp.bfloat16), fc1_weight, preferred_element_type=jnp.float32)
    activated, gelu_back = jax.vjp(gelu_exact, hidden_pre)
    activated_b = activated.astype(jnp.bfloat16)
    block_out = (mixed_rows + jnp.dot(activated_b, fc2_weight, preferred_element_type=jnp.float32)).astype(jnp.bfloat16)
    grad_act = jnp.dot(cotangent, fc2_weight.T, preferred_element_type=jnp.float32)
    grad_pre = gelu_back(grad_act)[0].astype(jnp.bfloat16)
    grad_normed = jnp.dot(grad_pre, fc1_weight.T, preferred_element_type=jnp.float32)
    grad_mixed = cotangent.astype(jnp.float32) + norm_back(grad_normed)[0]
    grad_attention = jnp.dot(grad_mixed.astype(jnp.bfloat16), proj_weight.T, preferred_element_type=jnp.float32).astype(jnp.bfloat16)
    return (block_out, grad_attention, grad_mixed)

def front_backward(ordered, grad_qkv, grad_mixed, norm1_gain, qkv_weight):
    unused, norm_back = jax.vjp(lambda row_block: norm_rows(row_block, norm1_gain), ordered.astype(jnp.float32))
    grad_normed = jnp.dot(grad_qkv.astype(jnp.bfloat16), qkv_weight.T, preferred_element_type=jnp.float32)
    return (grad_mixed + norm_back(grad_normed)[0]).astype(jnp.bfloat16)

def split_heads(matrix, head_count):
    return matrix.astype(jnp.float32).reshape(matrix.shape[0], head_count, matrix.shape[1] // head_count)

def attend(queries, key_rows, value_rows, head_count):
    row_count = queries.shape[0]
    head_size = queries.shape[1] // head_count
    score_scale = 1.0 / math.sqrt(head_size)
    query_heads = split_heads(queries, head_count)
    key_heads = split_heads(key_rows, head_count)
    value_heads = split_heads(value_rows, head_count)
    scores = jnp.einsum('qhd,khd->hqk', query_heads, key_heads) * score_scale
    weights = jnp.exp(scores)
    probs_b = (weights / lax.optimization_barrier(jnp.sum(weights, axis=-1, keepdims=True))).astype(jnp.bfloat16)
    result = jnp.einsum('hqk,khd->qhd', probs_b.astype(jnp.float32), value_heads)
    return result.reshape(row_count, -1).astype(jnp.bfloat16)

def attend_backward(queries, key_rows, value_rows, grad_out, head_count):
    row_count = queries.shape[0]
    window = key_rows.shape[0]
    head_size = queries.shape[1] // head_count
    score_scale = 1.0 / math.sqrt(head_size)
    query_heads = split_heads(queries, head_count)
    key_heads = split_heads(key_rows, head_count)
    value_heads = split_heads(value_rows, head_count)
    grad_heads = split_heads(grad_out, head_count)
    scores = jnp.einsum('qhd,khd->hqk', query_heads, key_heads) * score_scale
    weights = jnp.exp(scores)
    probs_full = weights / lax.optimization_barrier(jnp.sum(weights, axis=-1, keepdims=True))
    probs_b = probs_full.astype(jnp.bfloat16).astype(jnp.float32)
    grad_probs = jnp.einsum('qhd,khd->hqk', grad_heads, value_heads)
    grad_values = jnp.einsum('hqk,qhd->khd', probs_b, grad_heads)
    inner_sum = lax.optimization_barrier(jnp.sum(probs_full * grad_probs, axis=-1, keepdims=True))
    grad_scores = (probs_full * (grad_probs - inner_sum) * score_scale).astype(jnp.bfloat16).astype(jnp.float32)
    grad_queries = jnp.einsum('hqk,khd->qhd', grad_scores, key_heads)
    grad_keys = jnp.einsum('hqk,qhd->khd', grad_scores, query_heads)
    grad_window = jnp.concatenate([grad_keys.reshape(window, -1), grad_values.reshape(window, -1)], axis=1)
    return (grad_queries.reshape(row_count, -1), grad_window)

def by_blocks(matrix):
    return matrix.reshape((DEVICES, P_DEV) + matrix.shape[1:])

def unblock(matrix):
    return matrix.reshape((NPTS,) + matrix.shape[2:])

def reference(points, send_rows, recv_slot, norm1_gain, qkv_weight, proj_weight, norm2_gain, fc1_weight, fc2_weight, cotangent):
    outputs_list = []
    grads_list = []
    positions = jnp.arange(NPTS, dtype=jnp.int32)
    target = (positions // P_DEV).astype(jnp.int32)
    prev_dev = ((target - 1 + DEVICES) % DEVICES).astype(jnp.int32)
    next_dev = ((target + 1) % DEVICES).astype(jnp.int32)
    patch_count = NPTS // K
    for event_index in range(EVENTS):
        slot_ids = recv_slot[event_index].astype(jnp.int32)
        rows_table = send_rows[event_index]
        from_self = slot_ids < P_DEV
        from_prev = jnp.logical_and(slot_ids >= P_DEV, slot_ids < P_DEV + CAP)
        own_row = jnp.clip(slot_ids, 0, P_DEV - 1).astype(jnp.int32)
        prev_pos = jnp.clip(slot_ids - P_DEV, 0, CAP - 1).astype(jnp.int32)
        next_pos = jnp.clip(slot_ids - P_DEV - CAP, 0, CAP - 1).astype(jnp.int32)
        prev_row = rows_table[prev_dev, CAP + prev_pos]
        next_row = rows_table[next_dev, next_pos]
        curve_index = jnp.where(from_self, target * P_DEV + own_row, jnp.where(from_prev, prev_dev * P_DEV + prev_row, next_dev * P_DEV + next_row)).astype(jnp.int32)
        ordered = points[event_index][curve_index]
        qkv = unblock(lax.map(lambda row_block: front(row_block, norm1_gain, qkv_weight), by_blocks(ordered)))
        queries = qkv[:, :HD]
        key_values = qkv[:, HD:]
        rolled_q = jnp.roll(queries, SHIFT, axis=0).reshape(patch_count, K, HD)
        rolled_kv = jnp.roll(key_values, SHIFT, axis=0).reshape(patch_count, K, 2 * HD)
        attention = lax.map(lambda pair: attend(pair[0], pair[1][:, :HD], pair[1][:, HD:], H), (rolled_q, rolled_kv))
        attention = jnp.roll(attention.reshape(NPTS, HD), -SHIFT, axis=0)
        block_out, grad_attention, grad_mixed = lax.map(lambda trio: rest_pass(trio[0], trio[1], norm2_gain, proj_weight, fc1_weight, fc2_weight, trio[2]), (by_blocks(ordered), by_blocks(attention), by_blocks(cotangent[event_index])))
        block_out = unblock(block_out)
        grad_attention = unblock(grad_attention)
        grad_mixed = unblock(grad_mixed)
        rolled_g = jnp.roll(grad_attention, SHIFT, axis=0).reshape(patch_count, K, HD)
        grad_q, grad_kv = lax.map(lambda trio: attend_backward(trio[0], trio[1][:, :HD], trio[1][:, HD:], trio[2], H), (rolled_q, rolled_kv, rolled_g))
        grad_qkv = jnp.concatenate([grad_q.reshape(NPTS, HD), grad_kv.reshape(NPTS, 2 * HD)], axis=1)
        grad_qkv = jnp.roll(grad_qkv, -SHIFT, axis=0)
        grad_ordered = unblock(lax.map(lambda trio: front_backward(trio[0], trio[1], trio[2], norm1_gain, qkv_weight), (by_blocks(ordered), by_blocks(grad_qkv), by_blocks(grad_mixed))))
        grad_event = jnp.zeros((NPTS, C), jnp.bfloat16).at[curve_index].set(grad_ordered)
        outputs_list.append(block_out)
        grads_list.append(grad_event)
    return (jnp.stack(outputs_list), jnp.stack(grads_list))
```

```python
import functools
import math

import jax
import jax.numpy as jnp
from jax import lax
from jax.experimental import pallas as pl
from jax.experimental.pallas import tpu as pltpu
from jax.sharding import PartitionSpec as P

H = 16
SHIFT = 512
CHUNK = 256
EPS = 1e-05
AXES = ("gx", "gy")
F32 = jnp.float32
BF16 = jnp.bfloat16
VMEM = pl.BlockSpec(memory_space=pltpu.VMEM)


def mm(a, b):
    return lax.dot_general(a, b, (((1,), (0,)), ((), ())), preferred_element_type=F32)


def mm_t(a, b):
    return lax.dot_general(a, b, (((1,), (1,)), ((), ())), preferred_element_type=F32)


def normalize(rows):
    centered = rows - jnp.mean(rows, axis=-1, keepdims=True)
    inv = lax.rsqrt(jnp.mean(centered * centered, axis=-1, keepdims=True) + EPS)
    return centered * inv, inv


def normalize_back(unit, inv, grad):
    inner = jnp.mean(grad * unit, axis=-1, keepdims=True)
    return inv * (grad - jnp.mean(grad, axis=-1, keepdims=True) - unit * inner)


def as_column(row):
    wide = jnp.broadcast_to(row.astype(F32), (8, row.shape[1]))
    return wide.T[:, :1].astype(jnp.int32)


def pick(column, first, count):
    ids = lax.broadcasted_iota(jnp.int32, (column.shape[0], count), 1) + first
    return (column == ids).astype(F32).astype(BF16)


def place(row, first, count):
    ids = lax.broadcasted_iota(jnp.int32, (count, row.shape[1]), 0) + first
    return (row == ids).astype(F32).astype(BF16)


def outgoing_kernel(points_ref, send_ref, out_ref):
    out_ref[...] = mm(pick(as_column(send_ref[...]), 0, points_ref.shape[0]), points_ref[...]).astype(BF16)


def order_kernel(points_ref, prev_ref, next_ref, slot_ref, out_ref):
    rows, cap = points_ref.shape[0], prev_ref.shape[0]
    column = as_column(slot_ref[...])
    for start in range(0, rows, CHUNK):
        part = column[start : start + CHUNK]
        total = mm(pick(part, 0, rows), points_ref[...])
        total += mm(pick(part, rows, cap), prev_ref[...])
        total += mm(pick(part, rows + cap, cap), next_ref[...])
        out_ref[start : start + CHUNK, :] = total.astype(BF16)


def back_kernel(grad_ref, slot_ref, out_ref):
    out_ref[...] = mm(place(slot_ref[...], grad_ref.shape[0], out_ref.shape[0]), grad_ref[...]).astype(BF16)


def final_kernel(grad_ref, slot_ref, send_ref, prev_ref, next_ref, out_ref):
    rows, cap = grad_ref.shape[0], prev_ref.shape[0]
    for start in range(0, rows, CHUNK):
        total = mm(place(slot_ref[...], start, CHUNK), grad_ref[...])
        total += mm(place(send_ref[:, :cap], start, CHUNK), prev_ref[...])
        total += mm(place(send_ref[:, cap:], start, CHUNK), next_ref[...])
        out_ref[start : start + CHUNK, :] = total.astype(BF16)


def block_kernel(
    x_ref, cot_ref, gain1_ref, wqkv_ref, proj_ref, gain2_ref, fc1_ref, fc2_ref,
    out_ref, grad_ref,
    exps, q3, k3, v3, attn, recip, gext, gmixed, dqkv,
):
    rows, width = x_ref.shape
    hd = proj_ref.shape[0]
    head = hd // H
    scale = 1.0 / math.sqrt(head)
    starts = range(0, rows, CHUNK)
    wqkv_t = wqkv_ref[...].T
    tail = lax.broadcasted_iota(jnp.int32, (H, head, rows), 1)
    v3[:, head:, :] = jnp.where(tail < 2, 1.0, 0.0).astype(BF16)

    for start in starts:
        part = slice(start, start + CHUNK)
        unit, inv = normalize(x_ref[part, :].astype(F32))
        qkv = mm_t(wqkv_t, (unit * gain1_ref[...]).astype(BF16)).astype(BF16)
        q3[:, :, part] = (qkv[:hd].astype(F32) * scale).astype(BF16).reshape(H, head, CHUNK)
        k3[:, :, part] = qkv[hd : 2 * hd].reshape(H, head, CHUNK)
        v3[:, :head, part] = qkv[2 * hd :].reshape(H, head, CHUNK)

    def forward_head(h, carry):
        q_rows = q3[h].T
        v_rows = v3[h].T
        keys = k3[h]
        for start in starts:
            part = slice(start, start + CHUNK)
            weights = jnp.exp(mm(q_rows[part], keys)).astype(BF16)
            exps[h, part, :] = weights
            summed = mm(weights, v_rows).T
            inverse = 1.0 / summed[head : head + 1]
            attn[h, :, part] = summed[:head] * inverse
            recip[h, :, part] = inverse
        return carry

    lax.fori_loop(0, H, forward_head, 0)

    for start in starts:
        part = slice(start, start + CHUNK)
        attn_t = attn[:, :, part].reshape(hd, CHUNK)
        mixed = x_ref[part, :].astype(F32) + mm(attn_t.T.astype(BF16), proj_ref[...])
        unit, inv = normalize(mixed)
        pre = mm((unit * gain2_ref[...]).astype(BF16), fc1_ref[...])
        half = 0.5 + 0.5 * lax.erf(pre * math.sqrt(0.5))
        out_ref[part, :] = (mixed + mm((pre * half).astype(BF16), fc2_ref[...])).astype(BF16)
        slope = half + pre * (math.sqrt(0.5 / math.pi) * jnp.exp(-0.5 * pre * pre))
        cot = cot_ref[part, :]
        grad_pre = (mm_t(cot, fc2_ref[...]) * slope).astype(BF16)
        grad_normed = mm_t(grad_pre, fc1_ref[...]) * gain2_ref[...]
        grad_mixed = cot.astype(F32) + normalize_back(unit, inv, grad_normed)
        gmixed[part, :] = grad_mixed
        grad_attn = mm_t(proj_ref[...], grad_mixed.astype(BF16)).astype(BF16).astype(F32)
        inverse = recip[:, :, part]
        inner = jnp.sum((grad_attn * attn_t).reshape(H, head, CHUNK), axis=1, keepdims=True) * inverse
        inner_hi = inner.astype(BF16).astype(F32)
        gext[:, :head, part] = (grad_attn.reshape(H, head, CHUNK) * inverse).astype(BF16)
        which = lax.broadcasted_iota(jnp.int32, (H, head, CHUNK), 1)
        rest = jnp.where(which == 0, -inner_hi, jnp.where(which == 1, inner_hi - inner, 0.0))
        gext[:, head:, part] = rest.astype(BF16)

    def backward_head(h, carry):
        g_rows = gext[h].T
        k_rows = k3[h].T
        values = v3[h]
        grad_k = jnp.zeros((head, rows), F32)
        grad_v = jnp.zeros((head, rows), F32)
        for start in starts:
            part = slice(start, start + CHUNK)
            weights = exps[h, part, :]
            scores = (weights.astype(F32) * mm(g_rows[part], values)).astype(BF16)
            grad_v += mm(gext[h, :head, part], weights)
            grad_k += mm(q3[h, :, part], scores)
            dqkv[h, :, part] = (mm(scores, k_rows).T * scale).astype(BF16)
        dqkv[H + h] = grad_k.astype(BF16)
        dqkv[2 * H + h] = grad_v.astype(BF16)
        return carry

    lax.fori_loop(0, H, backward_head, 0)

    for start in starts:
        part = slice(start, start + CHUNK)
        grad_qkv = dqkv[:, :, part].reshape(3 * hd, CHUNK).astype(F32).T.astype(BF16)
        grad_normed = mm_t(grad_qkv, wqkv_ref[...]) * gain1_ref[...]
        unit, inv = normalize(x_ref[part, :].astype(F32))
        grad_ref[part, :] = (gmixed[part, :] + normalize_back(unit, inv, grad_normed)).astype(BF16)


def call(kernel, outs, args, scratch=(), vmem=32):
    return pl.pallas_call(
        kernel,
        out_shape=outs,
        in_specs=[VMEM] * len(args),
        out_specs=jax.tree.map(lambda leaf: VMEM, outs),
        scratch_shapes=list(scratch),
        compiler_params=pltpu.CompilerParams(vmem_limit_bytes=vmem * 2**20),
    )(*args)


def shards(points, send_rows, recv_slot, gain1, wqkv, proj, gain2, fc1, fc2, cotangent):
    rows, width = points.shape[1:]
    cap = send_rows.shape[2] // 2
    hd = proj.shape[0]
    head = hd // H
    count = lax.axis_size(AXES)
    up = [(i, (i + 1) % count) for i in range(count)]
    down = [((i + 1) % count, i) for i in range(count)]
    local, send, slot, cot = points[0], send_rows[0], recv_slot, cotangent[0]

    def like(*shape):
        return jax.ShapeDtypeStruct(shape, BF16)

    cot_half = lax.ppermute(cot[SHIFT:], AXES, up)
    outgoing = call(outgoing_kernel, like(2 * cap, width), (local, send))
    from_prev = lax.ppermute(outgoing[cap:], AXES, up)
    from_next = lax.ppermute(outgoing[:cap], AXES, down)
    ordered = call(order_kernel, like(rows, width), (local, from_prev, from_next, slot))
    half = lax.ppermute(ordered[SHIFT:], AXES, up)
    patch = jnp.concatenate([half, ordered[:SHIFT]], axis=0)
    patch_cot = jnp.concatenate([cot_half, cot[:SHIFT]], axis=0)
    patch_out, patch_grad = call(
        block_kernel,
        (like(rows, width), like(rows, width)),
        (patch, patch_cot, gain1[None], wqkv, proj, gain2[None], fc1, fc2),
        (
            pltpu.VMEM((H, rows, rows), BF16),
            pltpu.VMEM((H, head, rows), BF16),
            pltpu.VMEM((H, head, rows), BF16),
            pltpu.VMEM((H, 2 * head, rows), BF16),
            pltpu.VMEM((H, head, rows), F32),
            pltpu.VMEM((H, 1, rows), F32),
            pltpu.VMEM((H, 2 * head, rows), BF16),
            pltpu.VMEM((rows, width), F32),
            pltpu.VMEM((3 * H, head, rows), BF16),
        ),
        vmem=60,
    )
    block_out = jnp.concatenate([patch_out[SHIFT:], lax.ppermute(patch_out[:SHIFT], AXES, down)], axis=0)
    grad = jnp.concatenate([patch_grad[SHIFT:], lax.ppermute(patch_grad[:SHIFT], AXES, down)], axis=0)
    back = call(back_kernel, like(2 * cap, width), (grad, slot))
    back_prev = lax.ppermute(back[cap:], AXES, up)
    back_next = lax.ppermute(back[:cap], AXES, down)
    grad_points = call(final_kernel, like(rows, width), (grad, slot, send, back_prev, back_next))
    return block_out[None], grad_points[None]


def solution(mesh):
    split = P(None, AXES, None)
    in_specs = (split, split, P(None, AXES), P(), P(), P(), P(), P(), P(), split)
    return jax.shard_map(shards, mesh=mesh, in_specs=in_specs, out_specs=(split, split), check_vma=False)
```

```python
import functools
import math

import jax
import jax.numpy as jnp
from jax import lax
from jax.experimental import pallas as pl
from jax.experimental.pallas import tpu as pltpu
from jax.sharding import PartitionSpec as P

H = 16
SHIFT = 512
CHUNK = 256
EPS = 1e-05
AXES = ("gx", "gy")
F32 = jnp.float32
BF16 = jnp.bfloat16
VMEM = pl.BlockSpec(memory_space=pltpu.VMEM)
MESH = pl.DeviceIdType.MESH


def mm(a, b):
    return lax.dot_general(a, b, (((1,), (0,)), ((), ())), preferred_element_type=F32)


def mm_t(a, b):
    return lax.dot_general(a, b, (((1,), (1,)), ((), ())), preferred_element_type=F32)


def normalize(rows):
    centered = rows - jnp.mean(rows, axis=-1, keepdims=True)
    inv = lax.rsqrt(jnp.mean(centered * centered, axis=-1, keepdims=True) + EPS)
    return centered * inv, inv


def normalize_back(unit, inv, grad):
    inner = jnp.mean(grad * unit, axis=-1, keepdims=True)
    return inv * (grad - jnp.mean(grad, axis=-1, keepdims=True) - unit * inner)


def as_column(row):
    wide = jnp.broadcast_to(row.astype(F32), (8, row.shape[1]))
    return wide.T[:, :1].astype(jnp.int32)


def pick(column, first, count):
    ids = lax.broadcasted_iota(jnp.int32, (column.shape[0], count), 1) + first
    return (column == ids).astype(F32).astype(BF16)


def place(row, first, count):
    ids = lax.broadcasted_iota(jnp.int32, (count, row.shape[1]), 0) + first
    return (row == ids).astype(F32).astype(BF16)


def ring(sizes):
    major, minor = sizes
    count = major * minor
    me = lax.axis_index("gx") * minor + lax.axis_index("gy")
    right, left = lax.rem(me + 1, count), lax.rem(me + count - 1, count)
    return (right // minor, lax.rem(right, minor)), (left // minor, lax.rem(left, minor))


def greet(right, left):
    barrier = pltpu.get_barrier_semaphore()
    for neighbour in (left, right):
        pl.semaphore_signal(barrier, inc=1, device_id=neighbour, device_id_type=MESH)


def send_to(source, target, sems, index, device):
    copy = pltpu.make_async_remote_copy(
        src_ref=source,
        dst_ref=target,
        send_sem=sems.at[0, index],
        recv_sem=sems.at[1, index],
        device_id=device,
        device_id_type=MESH,
    )
    copy.start()
    return copy


def front_kernel(
    sizes, points_ref, send_ref, slot_ref, cot_ref, patch_ref, patch_cot_ref, outgoing, prev, next_, half, own, sems
):
    right, left = ring(sizes)
    greet(right, left)
    rows, cap = points_ref.shape[0], prev.shape[0]
    shift = half.shape[0]
    sender = as_column(send_ref[...])
    outgoing[cap:, :] = mm(pick(sender[cap:], 0, rows), points_ref[...]).astype(BF16)
    pl.semaphore_wait(pltpu.get_barrier_semaphore(), 2)
    to_right = send_to(outgoing.at[pl.ds(cap, cap)], prev, sems, 0, right)
    outgoing[:cap, :] = mm(pick(sender[:cap], 0, rows), points_ref[...]).astype(BF16)
    to_left = send_to(outgoing.at[pl.ds(0, cap)], next_, sems, 1, left)
    cot_copy = send_to(cot_ref.at[pl.ds(shift, shift)], patch_cot_ref.at[pl.ds(0, shift)], sems, 2, right)
    patch_cot_ref[shift:, :] = cot_ref[:shift, :]
    column = as_column(slot_ref[...])
    for start in range(0, rows, CHUNK):
        part = slice(start, start + CHUNK)
        own[part, :] = mm(pick(column[part], 0, rows), points_ref[...])
    to_right.wait_recv()
    to_left.wait_recv()

    def arrange(start):
        part = slice(start, start + CHUNK)
        total = own[part, :] + mm(pick(column[part], rows, cap), prev[...])
        return (total + mm(pick(column[part], rows + cap, cap), next_[...])).astype(BF16)

    for start in range(shift, rows, CHUNK):
        half[start - shift : start - shift + CHUNK, :] = arrange(start)
    half_copy = send_to(half, patch_ref.at[pl.ds(0, shift)], sems, 3, right)
    for start in range(0, shift, CHUNK):
        patch_ref[shift + start : shift + start + CHUNK, :] = arrange(start)
    to_right.wait_send()
    to_left.wait_send()
    cot_copy.wait()
    half_copy.wait()


def back_kernel(
    sizes, out_ref, grad_ref, slot_ref, send_ref, block_ref, points_ref, half, back, prev, next_, own, sems
):
    right, left = ring(sizes)
    greet(right, left)
    rows, cap = grad_ref.shape[0], prev.shape[0]
    shift = half.shape[0]
    pl.semaphore_wait(pltpu.get_barrier_semaphore(), 2)
    grad_copy = send_to(grad_ref.at[pl.ds(0, shift)], half, sems, 0, left)
    out_copy = send_to(out_ref.at[pl.ds(0, shift)], block_ref.at[pl.ds(shift, shift)], sems, 1, left)
    block_ref[:shift, :] = out_ref[shift:, :]
    first, second = slot_ref[:, :shift], slot_ref[:, shift:]
    mine = grad_ref[shift:, :]
    to_prev = mm(place(first, rows, cap), mine)
    to_next = mm(place(first, rows + cap, cap), mine)
    grad_copy.wait_recv()
    theirs = half[...]
    back[cap:, :] = (to_next + mm(place(second, rows + cap, cap), theirs)).astype(BF16)
    to_right = send_to(back.at[pl.ds(cap, cap)], prev, sems, 2, right)
    back[:cap, :] = (to_prev + mm(place(second, rows, cap), theirs)).astype(BF16)
    to_left = send_to(back.at[pl.ds(0, cap)], next_, sems, 3, left)
    for start in range(0, rows, CHUNK):
        total = mm(place(first, start, CHUNK), mine)
        own[start : start + CHUNK, :] = total + mm(place(second, start, CHUNK), theirs)
    to_right.wait_recv()
    to_left.wait_recv()
    for start in range(0, rows, CHUNK):
        total = own[start : start + CHUNK, :] + mm(place(send_ref[:, :cap], start, CHUNK), prev[...])
        total += mm(place(send_ref[:, cap:], start, CHUNK), next_[...])
        points_ref[start : start + CHUNK, :] = total.astype(BF16)
    grad_copy.wait_send()
    to_right.wait_send()
    to_left.wait_send()
    out_copy.wait()


def block_kernel(
    x_ref, cot_ref, gain1_ref, wqkv_ref, proj_ref, gain2_ref, fc1_ref, fc2_ref,
    out_ref, grad_ref,
    exps, q3, k3, v3, attn, recip, gext, gmixed, dqkv,
):
    rows, width = x_ref.shape
    hd = proj_ref.shape[0]
    head = hd // H
    scale = 1.0 / math.sqrt(head)
    starts = range(0, rows, CHUNK)
    wqkv_t = wqkv_ref[...].T
    tail = lax.broadcasted_iota(jnp.int32, (H, head, rows), 1)
    v3[:, head:, :] = jnp.where(tail < 2, 1.0, 0.0).astype(BF16)

    for start in starts:
        part = slice(start, start + CHUNK)
        unit, inv = normalize(x_ref[part, :].astype(F32))
        qkv = mm_t(wqkv_t, (unit * gain1_ref[...]).astype(BF16)).astype(BF16)
        q3[:, :, part] = (qkv[:hd].astype(F32) * scale).astype(BF16).reshape(H, head, CHUNK)
        k3[:, :, part] = qkv[hd : 2 * hd].reshape(H, head, CHUNK)
        v3[:, :head, part] = qkv[2 * hd :].reshape(H, head, CHUNK)

    def forward_head(h, carry):
        q_rows = q3[h].T
        v_rows = v3[h].T
        keys = k3[h]
        for start in starts:
            part = slice(start, start + CHUNK)
            weights = jnp.exp(mm(q_rows[part], keys)).astype(BF16)
            exps[h, part, :] = weights
            summed = mm(weights, v_rows).T
            inverse = 1.0 / summed[head : head + 1]
            attn[h, :, part] = summed[:head] * inverse
            recip[h, :, part] = inverse
        return carry

    lax.fori_loop(0, H, forward_head, 0, unroll=2)

    for start in starts:
        part = slice(start, start + CHUNK)
        attn_t = attn[:, :, part].reshape(hd, CHUNK)
        mixed = x_ref[part, :].astype(F32) + mm(attn_t.T.astype(BF16), proj_ref[...])
        unit, inv = normalize(mixed)
        pre = mm((unit * gain2_ref[...]).astype(BF16), fc1_ref[...])
        half = 0.5 + 0.5 * lax.erf(pre * math.sqrt(0.5))
        out_ref[part, :] = (mixed + mm((pre * half).astype(BF16), fc2_ref[...])).astype(BF16)
        slope = half + pre * (math.sqrt(0.5 / math.pi) * jnp.exp(-0.5 * pre * pre))
        cot = cot_ref[part, :]
        grad_pre = (mm_t(cot, fc2_ref[...]) * slope).astype(BF16)
        grad_normed = mm_t(grad_pre, fc1_ref[...]) * gain2_ref[...]
        grad_mixed = cot.astype(F32) + normalize_back(unit, inv, grad_normed)
        gmixed[part, :] = grad_mixed
        grad_attn = mm_t(proj_ref[...], grad_mixed.astype(BF16)).astype(BF16).astype(F32)
        inverse = recip[:, :, part]
        inner = jnp.sum((grad_attn * attn_t).reshape(H, head, CHUNK), axis=1, keepdims=True) * inverse
        inner_hi = inner.astype(BF16).astype(F32)
        gext[:, :head, part] = (grad_attn.reshape(H, head, CHUNK) * inverse).astype(BF16)
        which = lax.broadcasted_iota(jnp.int32, (H, head, CHUNK), 1)
        rest = jnp.where(which == 0, -inner_hi, jnp.where(which == 1, inner_hi - inner, 0.0))
        gext[:, head:, part] = rest.astype(BF16)

    def backward_head(h, carry):
        g_rows = gext[h].T
        k_rows = k3[h].T
        values = v3[h]
        grad_k = jnp.zeros((head, rows), F32)
        grad_v = jnp.zeros((head, rows), F32)
        for start in starts:
            part = slice(start, start + CHUNK)
            weights = exps[h, part, :]
            scores = (weights.astype(F32) * mm(g_rows[part], values)).astype(BF16)
            grad_v += mm(gext[h, :head, part], weights)
            grad_k += mm(q3[h, :, part], scores)
            dqkv[h, :, part] = (mm(scores, k_rows).T * scale).astype(BF16)
        dqkv[H + h] = grad_k.astype(BF16)
        dqkv[2 * H + h] = grad_v.astype(BF16)
        return carry

    lax.fori_loop(0, H, backward_head, 0, unroll=2)

    for start in starts:
        part = slice(start, start + CHUNK)
        grad_qkv = dqkv[:, :, part].reshape(3 * hd, CHUNK).astype(F32).T.astype(BF16)
        grad_normed = mm_t(grad_qkv, wqkv_ref[...]) * gain1_ref[...]
        unit, inv = normalize(x_ref[part, :].astype(F32))
        grad_ref[part, :] = (gmixed[part, :] + normalize_back(unit, inv, grad_normed)).astype(BF16)


def call(kernel, outs, args, scratch, vmem, collective=None):
    return pl.pallas_call(
        kernel,
        out_shape=outs,
        in_specs=[VMEM] * len(args),
        out_specs=jax.tree.map(lambda leaf: VMEM, outs),
        scratch_shapes=list(scratch),
        compiler_params=pltpu.CompilerParams(
            vmem_limit_bytes=vmem * 2**20, collective_id=collective, has_side_effects=collective is not None
        ),
    )(*args)


def shards(sizes, points, send_rows, recv_slot, gain1, wqkv, proj, gain2, fc1, fc2, cotangent):
    rows, width = points.shape[1:]
    cap = send_rows.shape[2] // 2
    hd = proj.shape[0]
    head = hd // H
    whole = jax.ShapeDtypeStruct((rows, width), BF16)
    send = send_rows[0]
    slots = pltpu.VMEM((cap, width), BF16)
    half = pltpu.VMEM((SHIFT, width), BF16)
    exchange = (
        pltpu.VMEM((2 * cap, width), BF16), slots, slots, half,
        pltpu.VMEM((rows, width), F32),
        pltpu.SemaphoreType.DMA((2, 4)),
    )
    patch, patch_cot = call(
        functools.partial(front_kernel, sizes),
        (whole, whole),
        (points[0], send, recv_slot, cotangent[0]),
        exchange,
        16,
        0,
    )
    patch_out, patch_grad = call(
        block_kernel,
        (whole, whole),
        (patch, patch_cot, gain1[None], wqkv, proj, gain2[None], fc1, fc2),
        (
            pltpu.VMEM((H, rows, rows), BF16),
            pltpu.VMEM((H, head, rows), BF16),
            pltpu.VMEM((H, head, rows), BF16),
            pltpu.VMEM((H, 2 * head, rows), BF16),
            pltpu.VMEM((H, head, rows), F32),
            pltpu.VMEM((H, 1, rows), F32),
            pltpu.VMEM((H, 2 * head, rows), BF16),
            pltpu.VMEM((rows, width), F32),
            pltpu.VMEM((3 * H, head, rows), BF16),
        ),
        60,
    )
    buffers, prev, next_, half, own, sems = exchange
    block_out, grad_points = call(
        functools.partial(back_kernel, sizes),
        (whole, whole),
        (patch_out, patch_grad, recv_slot, send),
        (half, buffers, prev, next_, own, sems),
        16,
        1,
    )
    return block_out[None], grad_points[None]


def solution(mesh):
    split = P(None, AXES, None)
    in_specs = (split, split, P(None, AXES), P(), P(), P(), P(), P(), P(), split)
    sizes = (mesh.shape["gx"], mesh.shape["gy"])
    return jax.shard_map(
        functools.partial(shards, sizes), mesh=mesh, in_specs=in_specs, out_specs=(split, split), check_vma=False
    )
```

```python
import functools
import math

import jax
import jax.numpy as jnp
from jax import lax
from jax.experimental import pallas as pl
from jax.experimental.pallas import tpu as pltpu
from jax.sharding import PartitionSpec as P

H = 16
SHIFT = 512
CHUNK = 256
EPS = 1e-05
AXES = ("gx", "gy")
F32 = jnp.float32
BF16 = jnp.bfloat16
VMEM = pl.BlockSpec(memory_space=pltpu.VMEM)
MESH = pl.DeviceIdType.MESH


def mm(a, b):
    return lax.dot_general(a, b, (((1,), (0,)), ((), ())), preferred_element_type=F32)


def mm_t(a, b):
    return lax.dot_general(a, b, (((1,), (1,)), ((), ())), preferred_element_type=F32)


def normalize(rows):
    centered = rows - jnp.mean(rows, axis=-1, keepdims=True)
    inv = lax.rsqrt(jnp.mean(centered * centered, axis=-1, keepdims=True) + EPS)
    return centered * inv, inv


def normalize_back(unit, inv, grad):
    inner = jnp.mean(grad * unit, axis=-1, keepdims=True)
    return inv * (grad - jnp.mean(grad, axis=-1, keepdims=True) - unit * inner)


def as_column(row):
    wide = jnp.broadcast_to(row.astype(F32), (8, row.shape[1]))
    return wide.T[:, :1].astype(jnp.int32)


def pick(column, first, count):
    ids = lax.broadcasted_iota(jnp.int32, (column.shape[0], count), 1) + first
    return (column == ids).astype(F32).astype(BF16)


def place(row, first, count):
    ids = lax.broadcasted_iota(jnp.int32, (count, row.shape[1]), 0) + first
    return (row == ids).astype(F32).astype(BF16)


def ring(sizes):
    major, minor = sizes
    count = major * minor
    me = lax.axis_index("gx") * minor + lax.axis_index("gy")
    right, left = lax.rem(me + 1, count), lax.rem(me + count - 1, count)
    return (right // minor, lax.rem(right, minor)), (left // minor, lax.rem(left, minor))


def greet(right, left):
    barrier = pltpu.get_barrier_semaphore()
    for neighbour in (left, right):
        pl.semaphore_signal(barrier, inc=1, device_id=neighbour, device_id_type=MESH)


def send_to(source, target, sems, index, device):
    copy = pltpu.make_async_remote_copy(
        src_ref=source,
        dst_ref=target,
        send_sem=sems.at[0, index],
        recv_sem=sems.at[1, index],
        device_id=device,
        device_id_type=MESH,
    )
    copy.start()
    return copy


def front_kernel(
    sizes, points_ref, send_ref, slot_ref, cot_ref, patch_ref, patch_cot_ref, outgoing, prev, next_, half, own, sems
):
    right, left = ring(sizes)
    greet(right, left)
    rows, cap = points_ref.shape[0], prev.shape[0]
    shift = half.shape[0]
    sender = as_column(send_ref[...])
    outgoing[cap:, :] = mm(pick(sender[cap:], 0, rows), points_ref[...]).astype(BF16)
    pl.semaphore_wait(pltpu.get_barrier_semaphore(), 2)
    to_right = send_to(outgoing.at[pl.ds(cap, cap)], prev, sems, 0, right)
    outgoing[:cap, :] = mm(pick(sender[:cap], 0, rows), points_ref[...]).astype(BF16)
    to_left = send_to(outgoing.at[pl.ds(0, cap)], next_, sems, 1, left)
    cot_copy = send_to(cot_ref.at[pl.ds(shift, shift)], patch_cot_ref.at[pl.ds(0, shift)], sems, 2, right)
    patch_cot_ref[shift:, :] = cot_ref[:shift, :]
    column = as_column(slot_ref[...])
    for start in range(0, rows, CHUNK):
        part = slice(start, start + CHUNK)
        own[part, :] = mm(pick(column[part], 0, rows), points_ref[...])
    to_right.wait_recv()
    to_left.wait_recv()

    def arrange(start):
        part = slice(start, start + CHUNK)
        total = own[part, :] + mm(pick(column[part], rows, cap), prev[...])
        return (total + mm(pick(column[part], rows + cap, cap), next_[...])).astype(BF16)

    for start in range(shift, rows, CHUNK):
        half[start - shift : start - shift + CHUNK, :] = arrange(start)
    half_copy = send_to(half, patch_ref.at[pl.ds(0, shift)], sems, 3, right)
    for start in range(0, shift, CHUNK):
        patch_ref[shift + start : shift + start + CHUNK, :] = arrange(start)
    to_right.wait_send()
    to_left.wait_send()
    cot_copy.wait()
    half_copy.wait()


def back_kernel(
    sizes, out_ref, grad_ref, slot_ref, send_ref, block_ref, points_ref, half, back, prev, next_, own, sems
):
    right, left = ring(sizes)
    greet(right, left)
    rows, cap = grad_ref.shape[0], prev.shape[0]
    shift = half.shape[0]
    pl.semaphore_wait(pltpu.get_barrier_semaphore(), 2)
    grad_copy = send_to(grad_ref.at[pl.ds(0, shift)], half, sems, 0, left)
    out_copy = send_to(out_ref.at[pl.ds(0, shift)], block_ref.at[pl.ds(shift, shift)], sems, 1, left)
    block_ref[:shift, :] = out_ref[shift:, :]
    first, second = slot_ref[:, :shift], slot_ref[:, shift:]
    mine = grad_ref[shift:, :]
    to_prev = mm(place(first, rows, cap), mine)
    to_next = mm(place(first, rows + cap, cap), mine)
    grad_copy.wait_recv()
    theirs = half[...]
    back[cap:, :] = (to_next + mm(place(second, rows + cap, cap), theirs)).astype(BF16)
    to_right = send_to(back.at[pl.ds(cap, cap)], prev, sems, 2, right)
    back[:cap, :] = (to_prev + mm(place(second, rows, cap), theirs)).astype(BF16)
    to_left = send_to(back.at[pl.ds(0, cap)], next_, sems, 3, left)
    for start in range(0, rows, CHUNK):
        total = mm(place(first, start, CHUNK), mine)
        own[start : start + CHUNK, :] = total + mm(place(second, start, CHUNK), theirs)
    to_right.wait_recv()
    to_left.wait_recv()
    for start in range(0, rows, CHUNK):
        total = own[start : start + CHUNK, :] + mm(place(send_ref[:, :cap], start, CHUNK), prev[...])
        total += mm(place(send_ref[:, cap:], start, CHUNK), next_[...])
        points_ref[start : start + CHUNK, :] = total.astype(BF16)
    grad_copy.wait_send()
    to_right.wait_send()
    to_left.wait_send()
    out_copy.wait()


def block_kernel(
    x_ref, cot_ref, gain1_ref, wqkv_ref, proj_ref, gain2_ref, fc1_ref, fc2_ref,
    out_ref, grad_ref,
    exps, q3, k3, v3, attn, recip, gext, gmixed, dqkv,
):
    rows, width = x_ref.shape
    hd = proj_ref.shape[0]
    head = hd // H
    scale = 1.0 / math.sqrt(head)
    starts = range(0, rows, CHUNK)
    wqkv_t = wqkv_ref[...].T
    tail = lax.broadcasted_iota(jnp.int32, (H, head, rows), 1)
    v3[:, head:, :] = jnp.where(tail < 2, 1.0, 0.0).astype(BF16)

    for start in starts:
        part = slice(start, start + CHUNK)
        unit, inv = normalize(x_ref[part, :].astype(F32))
        qkv = mm_t(wqkv_t, (unit * gain1_ref[...]).astype(BF16)).astype(BF16)
        q3[:, :, part] = (qkv[:hd].astype(F32) * scale).astype(BF16).reshape(H, head, CHUNK)
        k3[:, :, part] = qkv[hd : 2 * hd].reshape(H, head, CHUNK)
        v3[:, :head, part] = qkv[2 * hd :].reshape(H, head, CHUNK)

    def forward_head(h, carry):
        q_rows = q3[h].T
        values = v3[h]
        keys = k3[h]
        for start in starts:
            part = slice(start, start + CHUNK)
            weights = jnp.exp(mm(q_rows[part], keys)).astype(BF16)
            exps[h, part, :] = weights
            summed = mm_t(values, weights)
            inverse = 1.0 / summed[head : head + 1]
            attn[h, :, part] = summed[:head] * inverse
            recip[h, :, part] = inverse
        return carry

    lax.fori_loop(0, H, forward_head, 0, unroll=2)

    for start in starts:
        part = slice(start, start + CHUNK)
        attn_t = attn[:, :, part].reshape(hd, CHUNK)
        mixed = x_ref[part, :].astype(F32) + mm(attn_t.T.astype(BF16), proj_ref[...])
        unit, inv = normalize(mixed)
        pre = mm((unit * gain2_ref[...]).astype(BF16), fc1_ref[...])
        half = 0.5 + 0.5 * lax.erf(pre * math.sqrt(0.5))
        out_ref[part, :] = (mixed + mm((pre * half).astype(BF16), fc2_ref[...])).astype(BF16)
        slope = half + pre * (math.sqrt(0.5 / math.pi) * jnp.exp(-0.5 * pre * pre))
        cot = cot_ref[part, :]
        grad_pre = (mm_t(cot, fc2_ref[...]) * slope).astype(BF16)
        grad_normed = mm_t(grad_pre, fc1_ref[...]) * gain2_ref[...]
        grad_mixed = cot.astype(F32) + normalize_back(unit, inv, grad_normed)
        gmixed[part, :] = grad_mixed
        grad_attn = mm_t(proj_ref[...], grad_mixed.astype(BF16)).astype(BF16).astype(F32)
        inverse = recip[:, :, part]
        inner = jnp.sum((grad_attn * attn_t).reshape(H, head, CHUNK), axis=1, keepdims=True) * inverse
        inner_hi = inner.astype(BF16).astype(F32)
        gext[:, :head, part] = (grad_attn.reshape(H, head, CHUNK) * inverse).astype(BF16)
        which = lax.broadcasted_iota(jnp.int32, (H, head, CHUNK), 1)
        rest = jnp.where(which == 0, -inner_hi, jnp.where(which == 1, inner_hi - inner, 0.0))
        gext[:, head:, part] = rest.astype(BF16)

    def backward_head(h, carry):
        g_rows = gext[h].T
        keys = k3[h]
        values = v3[h]
        grad_k = jnp.zeros((head, rows), F32)
        grad_v = jnp.zeros((head, rows), F32)
        for start in starts:
            part = slice(start, start + CHUNK)
            weights = exps[h, part, :]
            scores = (weights.astype(F32) * mm(g_rows[part], values)).astype(BF16)
            grad_v += mm(gext[h, :head, part], weights)
            grad_k += mm(q3[h, :, part], scores)
            dqkv[h, :, part] = (mm_t(keys, scores) * scale).astype(BF16)
        dqkv[H + h] = grad_k.astype(BF16)
        dqkv[2 * H + h] = grad_v.astype(BF16)
        return carry

    lax.fori_loop(0, H, backward_head, 0, unroll=2)

    for start in starts:
        part = slice(start, start + CHUNK)
        grad_qkv = dqkv[:, :, part].reshape(3 * hd, CHUNK).astype(F32).T.astype(BF16)
        grad_normed = mm_t(grad_qkv, wqkv_ref[...]) * gain1_ref[...]
        unit, inv = normalize(x_ref[part, :].astype(F32))
        grad_ref[part, :] = (gmixed[part, :] + normalize_back(unit, inv, grad_normed)).astype(BF16)


def call(kernel, outs, args, scratch, vmem, collective=None):
    return pl.pallas_call(
        kernel,
        out_shape=outs,
        in_specs=[VMEM] * len(args),
        out_specs=jax.tree.map(lambda leaf: VMEM, outs),
        scratch_shapes=list(scratch),
        compiler_params=pltpu.CompilerParams(
            vmem_limit_bytes=vmem * 2**20, collective_id=collective, has_side_effects=collective is not None
        ),
    )(*args)


def shards(sizes, points, send_rows, recv_slot, gain1, wqkv, proj, gain2, fc1, fc2, cotangent):
    rows, width = points.shape[1:]
    cap = send_rows.shape[2] // 2
    hd = proj.shape[0]
    head = hd // H
    whole = jax.ShapeDtypeStruct((rows, width), BF16)
    send = send_rows[0]
    slots = pltpu.VMEM((cap, width), BF16)
    half = pltpu.VMEM((SHIFT, width), BF16)
    exchange = (
        pltpu.VMEM((2 * cap, width), BF16), slots, slots, half,
        pltpu.VMEM((rows, width), F32),
        pltpu.SemaphoreType.DMA((2, 4)),
    )
    patch, patch_cot = call(
        functools.partial(front_kernel, sizes),
        (whole, whole),
        (points[0], send, recv_slot, cotangent[0]),
        exchange,
        60,
        0,
    )
    patch_out, patch_grad = call(
        block_kernel,
        (whole, whole),
        (patch, patch_cot, gain1[None], wqkv, proj, gain2[None], fc1, fc2),
        (
            pltpu.VMEM((H, rows, rows), BF16),
            pltpu.VMEM((H, head, rows), BF16),
            pltpu.VMEM((H, head, rows), BF16),
            pltpu.VMEM((H, 2 * head, rows), BF16),
            pltpu.VMEM((H, head, rows), F32),
            pltpu.VMEM((H, 1, rows), F32),
            pltpu.VMEM((H, 2 * head, rows), BF16),
            pltpu.VMEM((rows, width), F32),
            pltpu.VMEM((3 * H, head, rows), BF16),
        ),
        60,
    )
    buffers, prev, next_, half, own, sems = exchange
    block_out, grad_points = call(
        functools.partial(back_kernel, sizes),
        (whole, whole),
        (patch_out, patch_grad, recv_slot, send),
        (half, buffers, prev, next_, own, sems),
        60,
        1,
    )
    return block_out[None], grad_points[None]


def solution(mesh):
    split = P(None, AXES, None)
    in_specs = (split, split, P(None, AXES), P(), P(), P(), P(), P(), P(), split)
    sizes = (mesh.shape["gx"], mesh.shape["gy"])
    return jax.shard_map(
        functools.partial(shards, sizes), mesh=mesh, in_specs=in_specs, out_specs=(split, split), check_vma=False
    )
```

```python
import functools
import math

import jax
import jax.numpy as jnp
from jax import lax
from jax.experimental import pallas as pl
from jax.experimental.pallas import tpu as pltpu
from jax.sharding import PartitionSpec as P

H = 16
SHIFT = 512
CHUNK = 256
EPS = 1e-05
AXES = ("gx", "gy")
F32 = jnp.float32
BF16 = jnp.bfloat16
VMEM = pl.BlockSpec(memory_space=pltpu.VMEM)
MESH = pl.DeviceIdType.MESH


def mm(a, b):
    return lax.dot_general(a, b, (((1,), (0,)), ((), ())), preferred_element_type=F32)


def mm_t(a, b):
    return lax.dot_general(a, b, (((1,), (1,)), ((), ())), preferred_element_type=F32)


def normalize(rows):
    centered = rows - jnp.mean(rows, axis=-1, keepdims=True)
    inv = lax.rsqrt(jnp.mean(centered * centered, axis=-1, keepdims=True) + EPS)
    return centered * inv, inv


def normalize_back(unit, inv, grad):
    inner = jnp.mean(grad * unit, axis=-1, keepdims=True)
    return inv * (grad - jnp.mean(grad, axis=-1, keepdims=True) - unit * inner)


def as_column(row):
    wide = jnp.broadcast_to(row.astype(F32), (8, row.shape[1]))
    return wide.T[:, :1].astype(jnp.int32)


def pick(column, first, count):
    ids = lax.broadcasted_iota(jnp.int32, (column.shape[0], count), 1) + first
    return (column == ids).astype(F32).astype(BF16)


def place(row, first, count):
    ids = lax.broadcasted_iota(jnp.int32, (count, row.shape[1]), 0) + first
    return (row == ids).astype(F32).astype(BF16)


def ring(sizes):
    major, minor = sizes
    count = major * minor
    me = lax.axis_index("gx") * minor + lax.axis_index("gy")
    right, left = lax.rem(me + 1, count), lax.rem(me + count - 1, count)
    return (right // minor, lax.rem(right, minor)), (left // minor, lax.rem(left, minor))


def greet(right, left):
    barrier = pltpu.get_barrier_semaphore()
    for neighbour in (left, right):
        pl.semaphore_signal(barrier, inc=1, device_id=neighbour, device_id_type=MESH)


def send_to(source, target, sems, index, device):
    copy = pltpu.make_async_remote_copy(
        src_ref=source,
        dst_ref=target,
        send_sem=sems.at[0, index],
        recv_sem=sems.at[1, index],
        device_id=device,
        device_id_type=MESH,
    )
    copy.start()
    return copy


def whole_kernel(
    sizes,
    points_ref, send_ref, slot_ref, cot_ref, gain1_ref, wqkv_ref, proj_ref, gain2_ref, fc1_ref, fc2_ref,
    block_ref, points_grad_ref,
    outgoing, prev, next_, half, own, x_ref, cot_half, leaving_out, leaving_grad, grad_half, mine_ref,
    back, back_prev, back_next,
    exps, q3, k3, v3, attn, recip, gext, gmixed, dqkv, sems,
):
    right, left = ring(sizes)
    greet(right, left)
    rows, cap = points_ref.shape[0], prev.shape[0]
    shift = half.shape[0]
    hd = proj_ref.shape[0]
    head = hd // H
    scale = 1.0 / math.sqrt(head)
    starts = range(0, rows, CHUNK)

    sender = as_column(send_ref[...])
    outgoing[cap:, :] = mm(pick(sender[cap:], 0, rows), points_ref[...]).astype(BF16)
    pl.semaphore_wait(pltpu.get_barrier_semaphore(), 2)
    to_right = send_to(outgoing.at[pl.ds(cap, cap)], prev, sems, 0, right)
    outgoing[:cap, :] = mm(pick(sender[:cap], 0, rows), points_ref[...]).astype(BF16)
    to_left = send_to(outgoing.at[pl.ds(0, cap)], next_, sems, 1, left)
    column = as_column(slot_ref[...])
    for start in starts:
        part = slice(start, start + CHUNK)
        own[part, :] = mm(pick(column[part], 0, rows), points_ref[...])
    wqkv_t = wqkv_ref[...].T
    tail = lax.broadcasted_iota(jnp.int32, (H, head, rows), 1)
    v3[:, head:, :] = jnp.where(tail < 2, 1.0, 0.0).astype(BF16)

    to_right.wait_recv()
    to_left.wait_recv()

    def arrange(start):
        part = slice(start, start + CHUNK)
        total = own[part, :] + mm(pick(column[part], rows, cap), prev[...])
        return (total + mm(pick(column[part], rows + cap, cap), next_[...])).astype(BF16)

    for start in range(shift, rows, CHUNK):
        half[start - shift : start - shift + CHUNK, :] = arrange(start)
    half_copy = send_to(half, x_ref.at[pl.ds(0, shift)], sems, 3, right)
    cot_copy = send_to(cot_ref.at[pl.ds(shift, shift)], cot_half, sems, 2, right)

    def project(start):
        part = slice(start, start + CHUNK)
        unit, inv = normalize(x_ref[part, :].astype(F32))
        qkv = mm_t(wqkv_t, (unit * gain1_ref[...]).astype(BF16)).astype(BF16)
        q3[:, :, part] = (qkv[:hd].astype(F32) * scale).astype(BF16).reshape(H, head, CHUNK)
        k3[:, :, part] = qkv[hd : 2 * hd].reshape(H, head, CHUNK)
        v3[:, :head, part] = qkv[2 * hd :].reshape(H, head, CHUNK)

    for start in range(0, shift, CHUNK):
        x_ref[shift + start : shift + start + CHUNK, :] = arrange(start)
    for start in range(shift, rows, CHUNK):
        project(start)
    half_copy.wait_recv()
    for start in range(0, shift, CHUNK):
        project(start)

    def forward_head(h, carry):
        q_rows = q3[h].T
        values = v3[h]
        keys = k3[h]
        for start in starts:
            part = slice(start, start + CHUNK)
            weights = jnp.exp(mm(q_rows[part], keys)).astype(BF16)
            exps[h, part, :] = weights
            summed = mm_t(values, weights)
            inverse = 1.0 / summed[head : head + 1]
            attn[h, :, part] = summed[:head] * inverse
            recip[h, :, part] = inverse
        return carry

    lax.fori_loop(0, H, forward_head, 0, unroll=2)

    cot_copy.wait_recv()
    for start in starts:
        part = slice(start, start + CHUNK)
        attn_t = attn[:, :, part].reshape(hd, CHUNK)
        mixed = x_ref[part, :].astype(F32) + mm(attn_t.T.astype(BF16), proj_ref[...])
        unit, inv = normalize(mixed)
        pre = mm((unit * gain2_ref[...]).astype(BF16), fc1_ref[...])
        cdf = 0.5 + 0.5 * lax.erf(pre * math.sqrt(0.5))
        block_out = (mixed + mm((pre * cdf).astype(BF16), fc2_ref[...])).astype(BF16)
        slope = cdf + pre * (math.sqrt(0.5 / math.pi) * jnp.exp(-0.5 * pre * pre))
        if start < shift:
            leaving_out[part, :] = block_out
            cot = cot_half[part, :]
        else:
            block_ref[start - shift : start - shift + CHUNK, :] = block_out
            cot = cot_ref[start - shift : start - shift + CHUNK, :]
        grad_pre = (mm_t(cot, fc2_ref[...]) * slope).astype(BF16)
        grad_normed = mm_t(grad_pre, fc1_ref[...]) * gain2_ref[...]
        grad_mixed = cot.astype(F32) + normalize_back(unit, inv, grad_normed)
        gmixed[part, :] = grad_mixed
        grad_attn = mm_t(proj_ref[...], grad_mixed.astype(BF16)).astype(BF16).astype(F32)
        inverse = recip[:, :, part]
        inner = jnp.sum((grad_attn * attn_t).reshape(H, head, CHUNK), axis=1, keepdims=True) * inverse
        inner_hi = inner.astype(BF16).astype(F32)
        gext[:, :head, part] = (grad_attn.reshape(H, head, CHUNK) * inverse).astype(BF16)
        which = lax.broadcasted_iota(jnp.int32, (H, head, CHUNK), 1)
        rest = jnp.where(which == 0, -inner_hi, jnp.where(which == 1, inner_hi - inner, 0.0))
        gext[:, head:, part] = rest.astype(BF16)
    out_copy = send_to(leaving_out, block_ref.at[pl.ds(shift, shift)], sems, 4, left)

    def backward_head(h, carry):
        g_rows = gext[h].T
        keys = k3[h]
        values = v3[h]
        grad_k = jnp.zeros((head, rows), F32)
        grad_v = jnp.zeros((head, rows), F32)
        for start in starts:
            part = slice(start, start + CHUNK)
            weights = exps[h, part, :]
            scores = (weights.astype(F32) * mm(g_rows[part], values)).astype(BF16)
            grad_v += mm(gext[h, :head, part], weights)
            grad_k += mm(q3[h, :, part], scores)
            dqkv[h, :, part] = (mm_t(keys, scores) * scale).astype(BF16)
        dqkv[H + h] = grad_k.astype(BF16)
        dqkv[2 * H + h] = grad_v.astype(BF16)
        return carry

    lax.fori_loop(0, H, backward_head, 0, unroll=2)

    def input_grad(start):
        part = slice(start, start + CHUNK)
        grad_qkv = dqkv[:, :, part].reshape(3 * hd, CHUNK).astype(F32).T.astype(BF16)
        grad_normed = mm_t(grad_qkv, wqkv_ref[...]) * gain1_ref[...]
        unit, inv = normalize(x_ref[part, :].astype(F32))
        return (gmixed[part, :] + normalize_back(unit, inv, grad_normed)).astype(BF16)

    for start in range(0, shift, CHUNK):
        leaving_grad[start : start + CHUNK, :] = input_grad(start)
    grad_copy = send_to(leaving_grad, grad_half, sems, 5, left)
    for start in range(shift, rows, CHUNK):
        mine_ref[start - shift : start - shift + CHUNK, :] = input_grad(start)

    first, second = slot_ref[:, :shift], slot_ref[:, shift:]
    mine = mine_ref[...]
    own[: 2 * cap, :] = mm(place(first, rows, 2 * cap), mine)
    grad_copy.wait_recv()
    theirs = grad_half[...]
    to_next = mm(place(second, rows + cap, cap), theirs)
    back[cap:, :] = (own[cap : 2 * cap, :] + to_next).astype(BF16)
    back_right = send_to(back.at[pl.ds(cap, cap)], back_prev, sems, 6, right)
    to_prev = mm(place(second, rows, cap), theirs)
    back[:cap, :] = (own[:cap, :] + to_prev).astype(BF16)
    back_left = send_to(back.at[pl.ds(0, cap)], back_next, sems, 7, left)
    for start in starts:
        total = mm(place(first, start, CHUNK), mine)
        own[start : start + CHUNK, :] = total + mm(place(second, start, CHUNK), theirs)
    to_right.wait_send()
    to_left.wait_send()
    half_copy.wait_send()
    cot_copy.wait_send()
    out_copy.wait()
    grad_copy.wait_send()
    back_right.wait_recv()
    back_left.wait_recv()
    for start in starts:
        total = own[start : start + CHUNK, :] + mm(place(send_ref[:, :cap], start, CHUNK), back_prev[...])
        total += mm(place(send_ref[:, cap:], start, CHUNK), back_next[...])
        points_grad_ref[start : start + CHUNK, :] = total.astype(BF16)
    back_right.wait_send()
    back_left.wait_send()


def shards(sizes, points, send_rows, recv_slot, gain1, wqkv, proj, gain2, fc1, fc2, cotangent):
    rows, width = points.shape[1:]
    cap = send_rows.shape[2] // 2
    hd = proj.shape[0]
    head = hd // H
    whole = jax.ShapeDtypeStruct((rows, width), BF16)
    args = (points[0], send_rows[0], recv_slot, cotangent[0], gain1[None], wqkv, proj, gain2[None], fc1, fc2)
    both = pltpu.VMEM((2 * cap, width), BF16)
    slots = pltpu.VMEM((cap, width), BF16)
    half = pltpu.VMEM((SHIFT, width), BF16)
    block_out, grad_points = pl.pallas_call(
        functools.partial(whole_kernel, sizes),
        out_shape=(whole, whole),
        in_specs=[VMEM] * len(args),
        out_specs=(VMEM, VMEM),
        scratch_shapes=[
            both, slots, slots, half,
            pltpu.VMEM((rows, width), F32),
            pltpu.VMEM((rows, width), BF16),
            half, half, half, half, half,
            both, slots, slots,
            pltpu.VMEM((H, rows, rows), BF16),
            pltpu.VMEM((H, head, rows), BF16),
            pltpu.VMEM((H, head, rows), BF16),
            pltpu.VMEM((H, 2 * head, rows), BF16),
            pltpu.VMEM((H, head, rows), F32),
            pltpu.VMEM((H, 1, rows), F32),
            pltpu.VMEM((H, 2 * head, rows), BF16),
            pltpu.VMEM((rows, width), F32),
            pltpu.VMEM((3 * H, head, rows), BF16),
            pltpu.SemaphoreType.DMA((2, 8)),
        ],
        compiler_params=pltpu.CompilerParams(
            vmem_limit_bytes=60 * 2**20, collective_id=0, has_side_effects=True
        ),
    )(*args)
    return block_out[None], grad_points[None]


def solution(mesh):
    split = P(None, AXES, None)
    in_specs = (split, split, P(None, AXES), P(), P(), P(), P(), P(), P(), split)
    sizes = (mesh.shape["gx"], mesh.shape["gy"])
    return jax.shard_map(
        functools.partial(shards, sizes), mesh=mesh, in_specs=in_specs, out_specs=(split, split), check_vma=False
    )
```

```python
import functools
import math

import jax
import jax.numpy as jnp
from jax import lax
from jax.experimental import pallas as pl
from jax.experimental.pallas import tpu as pltpu
from jax.sharding import PartitionSpec as P

H = 16
SHIFT = 512
CHUNK = 256
EPS = 1e-05
AXES = ("gx", "gy")
F32 = jnp.float32
BF16 = jnp.bfloat16
VMEM = pl.BlockSpec(memory_space=pltpu.VMEM)
MESH = pl.DeviceIdType.MESH


def mm(a, b):
    return lax.dot_general(a, b, (((1,), (0,)), ((), ())), preferred_element_type=F32)


def mm_t(a, b):
    return lax.dot_general(a, b, (((1,), (1,)), ((), ())), preferred_element_type=F32)


def normalize(rows):
    centered = rows - jnp.mean(rows, axis=-1, keepdims=True)
    inv = lax.rsqrt(jnp.mean(centered * centered, axis=-1, keepdims=True) + EPS)
    return centered * inv, inv


def normalize_back(unit, inv, grad):
    inner = jnp.mean(grad * unit, axis=-1, keepdims=True)
    return inv * (grad - jnp.mean(grad, axis=-1, keepdims=True) - unit * inner)


def as_column(row):
    wide = jnp.broadcast_to(row.astype(F32), (8, row.shape[1]))
    return wide.T[:, :1].astype(jnp.int32)


def pick(column, first, count):
    ids = lax.broadcasted_iota(jnp.int32, (column.shape[0], count), 1) + first
    return (column == ids).astype(F32).astype(BF16)


def place(row, first, count):
    ids = lax.broadcasted_iota(jnp.int32, (count, row.shape[1]), 0) + first
    return (row == ids).astype(F32).astype(BF16)


def ring(sizes):
    major, minor = sizes
    count = major * minor
    me = lax.axis_index("gx") * minor + lax.axis_index("gy")
    right, left = lax.rem(me + 1, count), lax.rem(me + count - 1, count)
    return (right // minor, lax.rem(right, minor)), (left // minor, lax.rem(left, minor))


def greet(right, left):
    barrier = pltpu.get_barrier_semaphore()
    for neighbour in (left, right):
        pl.semaphore_signal(barrier, inc=1, device_id=neighbour, device_id_type=MESH)


def send_to(source, target, sems, index, device):
    copy = pltpu.make_async_remote_copy(
        src_ref=source,
        dst_ref=target,
        send_sem=sems.at[0, index],
        recv_sem=sems.at[1, index],
        device_id=device,
        device_id_type=MESH,
    )
    copy.start()
    return copy


def whole_kernel(
    sizes,
    points_ref, send_ref, slot_ref, cot_ref, gain1_ref, wqkv_ref, proj_ref, gain2_ref, fc1_ref, fc2_ref,
    block_ref, points_grad_ref,
    outgoing, prev, next_, half, own, x_ref, cot_half, leaving_out, leaving_grad, grad_half, mine_ref,
    back, back_prev, back_next,
    exps, q3, k3, v3, attn, recip, gext, gmixed, dqkv, sems,
):
    right, left = ring(sizes)
    greet(right, left)
    rows, cap = points_ref.shape[0], prev.shape[0]
    shift = half.shape[0]
    hd = proj_ref.shape[0]
    head = hd // H
    scale = 1.0 / math.sqrt(head)
    starts = range(0, rows, CHUNK)

    sender = as_column(send_ref[...])
    outgoing[cap:, :] = mm(pick(sender[cap:], 0, rows), points_ref[...]).astype(BF16)
    pl.semaphore_wait(pltpu.get_barrier_semaphore(), 2)
    to_right = send_to(outgoing.at[pl.ds(cap, cap)], prev, sems, 0, right)
    outgoing[:cap, :] = mm(pick(sender[:cap], 0, rows), points_ref[...]).astype(BF16)
    to_left = send_to(outgoing.at[pl.ds(0, cap)], next_, sems, 1, left)
    column = as_column(slot_ref[...])
    for start in starts:
        part = slice(start, start + CHUNK)
        own[part, :] = mm(pick(column[part], 0, rows), points_ref[...])
    wqkv_t = wqkv_ref[...].T
    tail = lax.broadcasted_iota(jnp.int32, (H, head, rows), 1)
    v3[:, head:, :] = jnp.where(tail < 2, 1.0, 0.0).astype(BF16)

    to_right.wait_recv()
    to_left.wait_recv()

    def arrange(start):
        part = slice(start, start + CHUNK)
        total = own[part, :] + mm(pick(column[part], rows, cap), prev[...])
        return (total + mm(pick(column[part], rows + cap, cap), next_[...])).astype(BF16)

    for start in range(shift, rows, CHUNK):
        half[start - shift : start - shift + CHUNK, :] = arrange(start)
    half_copy = send_to(half, x_ref.at[pl.ds(0, shift)], sems, 3, right)
    cot_copy = send_to(cot_ref.at[pl.ds(shift, shift)], cot_half, sems, 2, right)

    def project(start):
        part = slice(start, start + CHUNK)
        unit, inv = normalize(x_ref[part, :].astype(F32))
        qkv = mm_t(wqkv_t, (unit * gain1_ref[...]).astype(BF16)).astype(BF16)
        q3[:, :, part] = (qkv[:hd].astype(F32) * scale).astype(BF16).reshape(H, head, CHUNK)
        k3[:, :, part] = qkv[hd : 2 * hd].reshape(H, head, CHUNK)
        v3[:, :head, part] = qkv[2 * hd :].reshape(H, head, CHUNK)

    for start in range(0, shift, CHUNK):
        x_ref[shift + start : shift + start + CHUNK, :] = arrange(start)
    for start in range(shift, rows, CHUNK):
        project(start)
    half_copy.wait_recv()
    for start in range(0, shift, CHUNK):
        project(start)

    def forward_head(h, carry):
        q_rows = q3[h].T
        values = v3[h]
        keys = k3[h]
        for start in starts:
            part = slice(start, start + CHUNK)
            weights = jnp.exp(mm(q_rows[part], keys)).astype(BF16)
            exps[h, part, :] = weights
            summed = mm_t(values, weights)
            inverse = 1.0 / summed[head : head + 1]
            attn[h, :, part] = summed[:head] * inverse
            recip[h, :, part] = inverse
        return carry

    lax.fori_loop(0, H, forward_head, 0, unroll=4)

    cot_copy.wait_recv()
    for start in starts:
        part = slice(start, start + CHUNK)
        attn_t = attn[:, :, part].reshape(hd, CHUNK)
        mixed = x_ref[part, :].astype(F32) + mm(attn_t.T.astype(BF16), proj_ref[...])
        unit, inv = normalize(mixed)
        pre = mm((unit * gain2_ref[...]).astype(BF16), fc1_ref[...])
        cdf = 0.5 + 0.5 * lax.erf(pre * math.sqrt(0.5))
        block_out = (mixed + mm((pre * cdf).astype(BF16), fc2_ref[...])).astype(BF16)
        slope = cdf + pre * (math.sqrt(0.5 / math.pi) * jnp.exp(-0.5 * pre * pre))
        if start < shift:
            leaving_out[part, :] = block_out
            cot = cot_half[part, :]
        else:
            block_ref[start - shift : start - shift + CHUNK, :] = block_out
            cot = cot_ref[start - shift : start - shift + CHUNK, :]
        grad_pre = (mm_t(cot, fc2_ref[...]) * slope).astype(BF16)
        grad_normed = mm_t(grad_pre, fc1_ref[...]) * gain2_ref[...]
        grad_mixed = cot.astype(F32) + normalize_back(unit, inv, grad_normed)
        gmixed[part, :] = grad_mixed
        grad_attn = mm_t(proj_ref[...], grad_mixed.astype(BF16)).astype(BF16).astype(F32)
        inverse = recip[:, :, part]
        inner = jnp.sum((grad_attn * attn_t).reshape(H, head, CHUNK), axis=1, keepdims=True) * inverse
        inner_hi = inner.astype(BF16).astype(F32)
        gext[:, :head, part] = (grad_attn.reshape(H, head, CHUNK) * inverse).astype(BF16)
        which = lax.broadcasted_iota(jnp.int32, (H, head, CHUNK), 1)
        rest = jnp.where(which == 0, -inner_hi, jnp.where(which == 1, inner_hi - inner, 0.0))
        gext[:, head:, part] = rest.astype(BF16)
    out_copy = send_to(leaving_out, block_ref.at[pl.ds(shift, shift)], sems, 4, left)

    def backward_head(h, carry):
        g_rows = gext[h].T
        keys = k3[h]
        values = v3[h]
        grad_k = jnp.zeros((head, rows), F32)
        grad_v = jnp.zeros((head, rows), F32)
        for start in starts:
            part = slice(start, start + CHUNK)
            weights = exps[h, part, :]
            scores = weights * mm(g_rows[part], values).astype(BF16)
            grad_v += mm(gext[h, :head, part], weights)
            grad_k += mm(q3[h, :, part], scores)
            dqkv[h, :, part] = (mm_t(keys, scores) * scale).astype(BF16)
        dqkv[H + h] = grad_k.astype(BF16)
        dqkv[2 * H + h] = grad_v.astype(BF16)
        return carry

    lax.fori_loop(0, H, backward_head, 0, unroll=4)

    def input_grad(start):
        part = slice(start, start + CHUNK)
        grad_qkv = dqkv[:, :, part].reshape(3 * hd, CHUNK).astype(F32).T.astype(BF16)
        grad_normed = mm_t(grad_qkv, wqkv_ref[...]) * gain1_ref[...]
        unit, inv = normalize(x_ref[part, :].astype(F32))
        return (gmixed[part, :] + normalize_back(unit, inv, grad_normed)).astype(BF16)

    for start in range(0, shift, CHUNK):
        leaving_grad[start : start + CHUNK, :] = input_grad(start)
    grad_copy = send_to(leaving_grad, grad_half, sems, 5, left)
    for start in range(shift, rows, CHUNK):
        mine_ref[start - shift : start - shift + CHUNK, :] = input_grad(start)

    first, second = slot_ref[:, :shift], slot_ref[:, shift:]
    mine = mine_ref[...]
    own[: 2 * cap, :] = mm(place(first, rows, 2 * cap), mine)
    grad_copy.wait_recv()
    theirs = grad_half[...]
    to_next = mm(place(second, rows + cap, cap), theirs)
    back[cap:, :] = (own[cap : 2 * cap, :] + to_next).astype(BF16)
    back_right = send_to(back.at[pl.ds(cap, cap)], back_prev, sems, 6, right)
    to_prev = mm(place(second, rows, cap), theirs)
    back[:cap, :] = (own[:cap, :] + to_prev).astype(BF16)
    back_left = send_to(back.at[pl.ds(0, cap)], back_next, sems, 7, left)
    for start in starts:
        total = mm(place(first, start, CHUNK), mine)
        own[start : start + CHUNK, :] = total + mm(place(second, start, CHUNK), theirs)
    to_right.wait_send()
    to_left.wait_send()
    half_copy.wait_send()
    cot_copy.wait_send()
    out_copy.wait()
    grad_copy.wait_send()
    back_right.wait_recv()
    back_left.wait_recv()
    for start in starts:
        total = own[start : start + CHUNK, :] + mm(place(send_ref[:, :cap], start, CHUNK), back_prev[...])
        total += mm(place(send_ref[:, cap:], start, CHUNK), back_next[...])
        points_grad_ref[start : start + CHUNK, :] = total.astype(BF16)
    back_right.wait_send()
    back_left.wait_send()


def shards(sizes, points, send_rows, recv_slot, gain1, wqkv, proj, gain2, fc1, fc2, cotangent):
    rows, width = points.shape[1:]
    cap = send_rows.shape[2] // 2
    hd = proj.shape[0]
    head = hd // H
    whole = jax.ShapeDtypeStruct((rows, width), BF16)
    args = (points[0], send_rows[0], recv_slot, cotangent[0], gain1[None], wqkv, proj, gain2[None], fc1, fc2)
    both = pltpu.VMEM((2 * cap, width), BF16)
    slots = pltpu.VMEM((cap, width), BF16)
    half = pltpu.VMEM((SHIFT, width), BF16)
    block_out, grad_points = pl.pallas_call(
        functools.partial(whole_kernel, sizes),
        out_shape=(whole, whole),
        in_specs=[VMEM] * len(args),
        out_specs=(VMEM, VMEM),
        scratch_shapes=[
            both, slots, slots, half,
            pltpu.VMEM((rows, width), F32),
            pltpu.VMEM((rows, width), BF16),
            half, half, half, half, half,
            both, slots, slots,
            pltpu.VMEM((H, rows, rows), BF16),
            pltpu.VMEM((H, head, rows), BF16),
            pltpu.VMEM((H, head, rows), BF16),
            pltpu.VMEM((H, 2 * head, rows), BF16),
            pltpu.VMEM((H, head, rows), F32),
            pltpu.VMEM((H, 1, rows), F32),
            pltpu.VMEM((H, 2 * head, rows), BF16),
            pltpu.VMEM((rows, width), F32),
            pltpu.VMEM((3 * H, head, rows), BF16),
            pltpu.SemaphoreType.DMA((2, 8)),
        ],
        compiler_params=pltpu.CompilerParams(
            vmem_limit_bytes=60 * 2**20, collective_id=0, has_side_effects=True
        ),
    )(*args)
    return block_out[None], grad_points[None]


def solution(mesh):
    split = P(None, AXES, None)
    in_specs = (split, split, P(None, AXES), P(), P(), P(), P(), P(), P(), split)
    sizes = (mesh.shape["gx"], mesh.shape["gy"])
    return jax.shard_map(
        functools.partial(shards, sizes), mesh=mesh, in_specs=in_specs, out_specs=(split, split), check_vma=False
    )
```
